512 devices in a mesh: seq: 64 (over y, z_hi, core), head: 8 (over x, z_lo).
Axes of the slice: x: 4, y: 8, z: 8 (z_hi: 4, z_lo: 2; z = z_hi * 2 + z_lo), core: 2. Of those that a mesh axis runs over, the one named last changes fastest.
Arguments:
- query_rows: bfloat16 [16384, 3072], P(('seq', 'head')), may hold values from -16 to 16
- key_rows: bfloat16 [16384, 1024], P(('seq', 'head')), may hold values from -16 to 16
- value_rows: bfloat16 [16384, 1024], P(('seq', 'head')), may hold values from -6 to 6
- residual: bfloat16 [16384, 3072], P(('seq', 'head')), may hold values from -6 to 6
- out_weight: bfloat16 [3072, 3072], P('head'), may hold values from -0.109375 to 0.109375
- gate_table: float32 [64, 3072], replicated, may hold values from -4 to 4
- noise_steps: int32 [8], replicated, may hold values from 0 to 63
- segment_mask: int32 [8, 8], replicated, may hold values from 0 to 1, as said below
- segment_map: int32 [64], replicated, may hold values from 0 to 7, as said below
Outputs:
- layer_output: bfloat16 [16384, 3072], P(('seq', 'head'))
The draws below stay inside these ranges and needn't reach their ends.
Inputs may be any that keep to these rules, and one draw needn't show every extreme that they name: `segment_mask`: ones on the diagonal, zeros above it. `segment_map`: each segment number stands in exactly 8 entries.
All inputs are finite; a program needn't handle non-finite values.
Results may differ from the reference program's by a relative error of at most 0.0095.
Values may be sent and summed in bfloat16 or wider, within the bound.
A program may use at most 64 MiB of HBM per device.

```python
import math
import jax
import jax.numpy as jnp
from jax import lax

Q_HEADS = 24
KV_HEADS = 8
HEAD_DIM = 128
D = 3072
TOK_DEV = 256
SEGMENTS = 8
STEPS = 64
SEG_DEVS = 8
TOKENS = 16384


def draw_query_rows(key, part):
    key = jax.random.fold_in(key, 11)
    drawn = 1.5 * jnp.clip(jax.random.normal(key, (TOKENS, D), jnp.float32), -6.0, 6.0)
    return drawn.astype(jnp.bfloat16)


def draw_key_rows(key, part):
    key = jax.random.fold_in(key, 13)
    drawn = 2.5 * jnp.clip(jax.random.normal(key, (TOKENS, KV_HEADS * HEAD_DIM), jnp.float32), -6.0, 6.0)
    return drawn.astype(jnp.bfloat16)


def draw_segment_mask(key, part):
    key = jax.random.fold_in(key, 17)
    coins = jax.random.randint(key, (SEGMENTS, SEGMENTS), 0, 4)
    later = jnp.arange(SEGMENTS, dtype=jnp.int32)[:, None]
    earlier = jnp.arange(SEGMENTS, dtype=jnp.int32)[None, :]
    return jnp.where(later == earlier, 1, jnp.where(earlier < later, (coins > 0).astype(jnp.int32), 0)).astype(jnp.int32)


def draw_segment_map(key, part):
    key = jax.random.fold_in(key, 19)
    return (jax.random.permutation(key, SEGMENTS * SEG_DEVS) // SEG_DEVS).astype(jnp.int32)


def with_ends(values, key, low, largest):
    place = [jax.random.randint(jax.random.fold_in(key, axis), (), 0, length) for axis, length in enumerate(values.shape)]
    widest = values.shape.index(max(values.shape))
    next_to = place[:widest] + [(place[widest] + 1) % values.shape[widest]] + place[widest + 1:]
    return values.at[tuple(place)].set(low).at[tuple(next_to)].set(largest)


def block_scale(rng, dims, split, least, top_value):
    def one(dim, parts):
        heights = jax.random.uniform(jax.random.fold_in(jax.random.fold_in(rng, 6), dim), (parts,), jnp.float32, least / len(split), top_value / len(split))
        return jnp.repeat(jnp.exp(heights), dims[dim] // parts).reshape((-1,) + (1,) * (len(dims) - dim - 1))

    level = one(*split[0])
    for cut in split[1:]:
        level = level * one(*cut)
    return level


def scatter_about(rng, dims, width, reach, shards=(), held_as=jnp.bfloat16):
    values = width * jax.random.normal(rng, dims, jnp.float32)
    if shards:
        values = values * block_scale(rng, dims, shards, -0.22, 0.18)
    return jnp.clip(values, -reach, reach).astype(held_as)


def setup_inputs(seed: int = 0) -> dict:
    keys = jax.random.split(jax.random.key(seed), 10)
    query_rows = draw_query_rows(jax.random.fold_in(keys[9], 71), 0)
    key_rows = draw_key_rows(jax.random.fold_in(keys[9], 71), 0)
    value_rows = scatter_about(keys[2], (TOKENS, KV_HEADS * HEAD_DIM), 1.0, 6.0, ((0, 512),))
    residual = scatter_about(keys[3], (TOKENS, D), 1.0, 6.0, ((0, 512),))
    out_weight = scatter_about(keys[4], (D, D), D ** -0.5, 0.109375, ((0, 8),))
    gate_table = scatter_about(keys[5], (STEPS, D), 1.0, 4.0, (), jnp.float32)
    noise_steps = with_ends(jax.random.randint(keys[6], (SEGMENTS,), 0, STEPS), jax.random.fold_in(keys[6], 1), 0, STEPS - 1).astype(jnp.int32)
    segment_mask = draw_segment_mask(jax.random.fold_in(keys[9], 71), 0)
    segment_map = draw_segment_map(jax.random.fold_in(keys[9], 71), 0)
    return dict(query_rows=query_rows, key_rows=key_rows, value_rows=value_rows, residual=residual, out_weight=out_weight, gate_table=gate_table, noise_steps=noise_steps, segment_mask=segment_mask, segment_map=segment_map)


NEG = -1.0e30


def reference(query_rows, key_rows, value_rows, residual, out_weight, gate_table, noise_steps, segment_mask, segment_map):
    tokens = query_rows.shape[0]
    group_size = Q_HEADS // KV_HEADS
    token_segment = segment_map[jnp.arange(tokens, dtype=jnp.int32) // TOK_DEV].astype(jnp.int32)
    key_all = key_rows.astype(jnp.float32).reshape(tokens, KV_HEADS, HEAD_DIM)
    value_all = value_rows.astype(jnp.float32).reshape(tokens, KV_HEADS, HEAD_DIM)
    query_all = query_rows.astype(jnp.float32).reshape(tokens, KV_HEADS, group_size, HEAD_DIM)
    block_size = math.gcd(tokens, 128)

    def attend(position):
        start_row = (position * block_size).astype(jnp.int32)
        query_blk = lax.dynamic_slice_in_dim(query_all, start_row, block_size, 0)
        segment_blk = lax.dynamic_slice_in_dim(token_segment, start_row, block_size, 0)
        visible = segment_mask[segment_blk][:, token_segment] > 0
        scores = jnp.einsum("qcgd,kcd->cgqk", query_blk, key_all, precision=lax.Precision.HIGHEST) * (HEAD_DIM ** -0.5)
        scores = jnp.where(visible[None, None], scores, NEG)
        row_max = jnp.max(scores, axis=-1, keepdims=True)
        weights = jnp.where(visible[None, None], jnp.exp(scores - row_max), 0.0)
        weight_sum = jnp.sum(weights, axis=-1)
        rounded = lax.optimization_barrier(weights.astype(jnp.bfloat16)).astype(jnp.float32)
        mixed = jnp.einsum("cgqk,kcd->cgqd", rounded, value_all, precision=lax.Precision.HIGHEST) / weight_sum[..., None]
        return jnp.transpose(mixed, (2, 0, 1, 3)).reshape(block_size, Q_HEADS * HEAD_DIM).astype(jnp.bfloat16)

    attended = lax.map(attend, jnp.arange(tokens // block_size, dtype=jnp.int32)).reshape(tokens, Q_HEADS * HEAD_DIM)
    projected = jnp.dot(attended, out_weight, preferred_element_type=jnp.float32)
    gate_rows = gate_table[noise_steps[token_segment]]
    return (residual.astype(jnp.float32) + gate_rows * projected).astype(jnp.bfloat16)
```

```python
import functools

import jax
import jax.numpy as jnp
from jax import lax
from jax.experimental import pallas as pl
from jax.experimental.pallas import tpu as pltpu
from jax.sharding import PartitionSpec as P

HEAD_DIM = 128
GROUP = 3
GW = GROUP * HEAD_DIM
NZ = 4
NC = 2
MASKED = -1e30
FLOOR = -1e20
SCALE = 1.4426950408889634 / HEAD_DIM**0.5
MESH = pl.DeviceIdType.MESH
CHUNK = 1024


def nt_dot(a, b):
    return lax.dot_general(a, b, (((1,), (1,)), ((), ())), preferred_element_type=jnp.float32)


def kernel(
    ny, nh, rows,
    q_hbm, k_hbm, v_hbm, res_hbm, w_hbm, gate_hbm, steps_ref, mask_ref, map_ref,
    out_ref,
    kv, q_all, scores, mx_acc, mx, acc, stat, stat_send, stat_recv, o_own, o_send, o_recv,
    attended, w_v, gate_v, res_v, part, part_recv, bias,
    k_ss, k_rs, v_ss, v_rs, q_ss, q_rs, right_ss, right_rs, left_ss, left_rs,
    sib_ss, sib_rs, o_ss, o_rs, st_ss, st_rs, p_ss, p_rs, loc,
):
    seq = lax.axis_index("seq")
    head = lax.axis_index("head")
    core = lax.rem(seq, NC)
    zh = lax.rem(seq // NC, NZ)
    y = seq // (NC * NZ)
    tok = rows * nh
    n_slots = 2 * ny

    def place(py, pz, pc):
        return (py * NZ + pz) * NC + pc

    def at_head(d):
        return lax.rem(head + d, nh)

    def at_z(d):
        return lax.rem(zh + d, NZ)

    def at_y(d):
        return lax.rem(y + d + ny, ny)

    def dev(s, h):
        return {"seq": s, "head": h}

    other = place(y, zh, 1 - core)
    right = place(at_y(1), zh, core)
    left = place(at_y(-1), zh, core)

    barrier = pltpu.get_barrier_semaphore()
    for dz in range(NZ):
        for dh in range(nh):
            if dz or dh:
                pl.semaphore_signal(
                    barrier, inc=1, device_id=dev(place(y, at_z(dz), core), at_head(dh)), device_id_type=MESH
                )
    for target in (other, right, left):
        pl.semaphore_signal(barrier, inc=1, device_id=dev(target, head), device_id_type=MESH)

    def cols(h, width):
        return pl.ds(pl.multiple_of(h * width, HEAD_DIM), width)

    def own_rows(h):
        return pl.ds(pl.multiple_of(h * rows, rows), rows)

    local = [
        pltpu.make_async_copy(k_hbm.at[:, cols(head, HEAD_DIM)], kv.at[own_rows(head), 0:128], loc.at[0]),
        pltpu.make_async_copy(v_hbm.at[:, cols(head, HEAD_DIM)], kv.at[own_rows(head), 128:256], loc.at[1]),
        pltpu.make_async_copy(q_hbm.at[:, cols(head, GW)], q_all.at[0, own_rows(head)], loc.at[2]),
        pltpu.make_async_copy(w_hbm, w_v, loc.at[3]),
        pltpu.make_async_copy(gate_hbm, gate_v, loc.at[4]),
        pltpu.make_async_copy(res_hbm, res_v, loc.at[5]),
    ]
    for cp in local[:3]:
        cp.start()

    def fill(i, carry):
        d = i // n_slots
        j = lax.rem(i, n_slots)
        q_seg = map_ref[place(y, at_z(d), core)]
        k_seg = map_ref[place(at_y(j // 2), zh, lax.rem(core + j, 2))]
        bias[i] = jnp.where(mask_ref[q_seg, k_seg] > 0, 0.0, MASKED).astype(jnp.float32)
        return carry

    lax.fori_loop(0, NZ * n_slots, fill, 0)

    pl.semaphore_wait(barrier, NZ * nh - 1 + 3)

    sends = []

    def remote(src, dst, ss, rs, target):
        cp = pltpu.make_async_remote_copy(
            src_ref=src, dst_ref=dst, send_sem=ss, recv_sem=rs, device_id=target, device_id_type=MESH
        )
        cp.start()
        sends.append(cp)
        return cp

    kv_in = []
    for d in range(1, nh):
        target = dev(seq, at_head(d))
        kv_in.append(remote(k_hbm.at[:, cols(at_head(d), HEAD_DIM)], kv.at[own_rows(head), 0:128],
                            k_ss.at[d], k_rs.at[d], target))
        kv_in.append(remote(v_hbm.at[:, cols(at_head(d), HEAD_DIM)], kv.at[own_rows(head), 128:256],
                            v_ss.at[d], v_rs.at[d], target))
    q_in = {s: [] for s in range(NZ)}
    for dz in (0, 1, 3, 2):
        if dz >= NZ:
            continue
        slot = (NZ - dz) % NZ
        for dh in range(nh):
            if dz or dh:
                i = dz * nh + dh
                q_in[slot].append(remote(q_hbm.at[:, cols(at_head(dh), GW)], q_all.at[slot, own_rows(head)],
                                         q_ss.at[i], q_rs.at[i], dev(place(y, at_z(dz), core), at_head(dh))))
    for cp in local[3:]:
        cp.start()

    def ones(i, carry):
        kv[pl.ds(pl.multiple_of(i * 256, 256), 256), 256:384] = jnp.ones((256, 128), jnp.bfloat16)
        return carry

    lax.fori_loop(0, n_slots * tok // 256, ones, 0)

    local[0].wait()
    local[1].wait()
    for cp in kv_in:
        cp.wait_recv()

    def block(r, c, lo=0, hi=256):
        return kv.at[pl.ds((r * 2 + c) * tok, tok), lo:hi]

    half = ny // 2
    sib = []

    def pass_on(r):
        sib.append(remote(block(r, 0), block(r, 1), sib_ss.at[r], sib_rs.at[r], dev(other, head)))

    r_in = l_in = None
    for s in range(half + 1):
        if s:
            r_in.wait_recv()
            l_in.wait_recv()
        if s < half:
            lo, hi = (0, 256) if s < half - 1 else (0, 128)
            lo2, hi2 = (0, 256) if s < half - 1 else (128, 256)
            r_in = remote(block((ny - s) % ny, 0, lo, hi), block((ny - s - 1) % ny, 0, lo, hi),
                          right_ss.at[s], right_rs.at[s], dev(right, head))
            l_in = remote(block(s, 0, lo2, hi2), block(s + 1, 0, lo2, hi2),
                          left_ss.at[s], left_rs.at[s], dev(left, head))
        pass_on(s)
        if 0 < s < half:
            pass_on(ny - s)
    for cp in sib:
        cp.wait_recv()
    local[2].wait()
    for cp in q_in[0]:
        cp.wait_recv()

    n_chunks = n_slots * tok // CHUNK if n_slots * tok >= CHUNK else 1
    width = n_slots * tok // n_chunks
    per = width // tok

    def key_rows_of(jc):
        return pl.ds(pl.multiple_of(jc * width, 128), width)

    def first(jc, q_tile, d, buf):
        s = nt_dot(q_tile, kv[key_rows_of(jc), 0:128])
        scores[buf, :, key_rows_of(jc)] = s
        m = mx_acc[...]
        for b in range(per):
            off = bias[d * n_slots + jc * per + b]
            for e in range(tok // 128):
                at = b * tok + e * 128
                m = jnp.maximum(m, s[:, at:at + 128] + off)
        mx_acc[...] = m

    def second(jc, d, buf):
        m = mx[...]
        pieces = []
        s = scores[buf, :, key_rows_of(jc)]
        for b in range(per):
            shift = (bias[d * n_slots + jc * per + b] - m) * SCALE
            for e in range(tok // 128):
                at = b * tok + e * 128
                pieces.append(jnp.exp2(s[:, at:at + 128] * SCALE + shift).astype(jnp.bfloat16))
        p = jnp.concatenate(pieces, axis=1)
        acc[...] += jnp.dot(p, kv[key_rows_of(jc), 128:384], preferred_element_type=jnp.float32)

    def close_first():
        mx[...] = jnp.broadcast_to(jnp.max(mx_acc[...], axis=1, keepdims=True), (tok, 128))
        mx_acc[...] = jnp.full((tok, 128), FLOOR, jnp.float32)
        acc[...] = jnp.zeros((tok, 256), jnp.float32)

    order = [s for s in (0, 1, 3, 2) if s < NZ]
    tiles = [(d, g) for d in order for g in range(GROUP)]
    lane = lax.broadcasted_iota(jnp.int32, (tok, 128), 1)

    mx_acc[...] = jnp.full((tok, 128), FLOOR, jnp.float32)

    def start_tile(d, g):
        return q_all[d, :, g * 128:(g + 1) * 128]

    q_tile = start_tile(*tiles[0])

    def only_first(jc, carry):
        first(jc, q_tile, tiles[0][0], 0)
        return carry

    lax.fori_loop(0, n_chunks, only_first, 0)
    close_first()
    o_in = {}
    for t, (d, g) in enumerate(tiles):
        buf = t % 2
        more = t + 1 < len(tiles)
        if more:
            nd, ng = tiles[t + 1]
            if ng == 0:
                for cp in q_in[nd]:
                    cp.wait_recv()
            q_next = start_tile(nd, ng)

        def both(jc, carry):
            second(jc, d, buf)
            if more:
                first(jc, q_next, nd, 1 - buf)
            return carry

        lax.fori_loop(0, n_chunks, both, 0)
        total = jnp.maximum(acc[:, 128:256], 1e-30)
        value = acc[:, 0:128] / total
        level = mx[...] * SCALE + jnp.log2(total)
        stat[...] = jnp.where(lane == g, level, stat[...]) if g else level
        if d == 0:
            o_own[:, g * 128:(g + 1) * 128] = value
        else:
            o_send[d - 1, :, g * 128:(g + 1) * 128] = value.astype(jnp.bfloat16)
        if g == GROUP - 1:
            if d == 0:
                stat_recv[0] = jnp.transpose(stat[...])[0:8]
            else:
                slot = (NZ - d) % NZ
                stat_send[d - 1] = jnp.transpose(stat[...])[0:8]
                target = dev(place(y, at_z(d), core), head)
                o_in[slot] = (
                    remote(o_send.at[d - 1], o_recv.at[slot - 1], o_ss.at[d - 1], o_rs.at[d - 1], target),
                    remote(stat_send.at[d - 1], stat_recv.at[slot], st_ss.at[d - 1], st_rs.at[d - 1], target),
                )
        if more:
            close_first()

    for slot in o_in:
        for cp in o_in[slot]:
            cp.wait_recv()
    zeros = jnp.zeros((120, tok), jnp.float32)
    levels = [jnp.transpose(jnp.concatenate([stat_recv[i], zeros], axis=0)) for i in range(NZ)]
    top = functools.reduce(jnp.maximum, levels)
    shares = [jnp.exp2(v - top) for v in levels]
    whole = functools.reduce(jnp.add, shares)
    shares = [v / whole for v in shares]
    for g in range(GROUP):
        at = slice(g * 128, (g + 1) * 128)
        mixed = shares[0][:, g:g + 1] * o_own[:, at]
        for i in range(1, NZ):
            mixed += shares[i][:, g:g + 1] * o_recv[i - 1, :, at].astype(jnp.float32)
        attended[:, at] = mixed.astype(jnp.bfloat16)

    local[3].wait()
    n_cols = w_v.shape[1]
    width_p = min(CHUNK, n_cols)
    p_in = []
    for ci in range(n_cols // width_p):
        at = slice(ci * width_p, (ci + 1) * width_p)
        part[:, at] = jnp.dot(attended[...], w_v[:, at], preferred_element_type=jnp.float32).astype(jnp.bfloat16)
        row = []
        for d in range(1, nh):
            to = at_head(d)
            row.append(remote(part.at[own_rows(to), at], part_recv.at[d - 1, :, at],
                              p_ss.at[ci * nh + d], p_rs.at[ci * nh + d], dev(seq, to)))
        p_in.append(row)
    local[4].wait()
    local[5].wait()
    step = steps_ref[map_ref[seq]]
    for ci in range(n_cols // width_p):
        at = slice(ci * width_p, (ci + 1) * width_p)
        for cp in p_in[ci]:
            cp.wait_recv()
        summed = part[own_rows(head), at].astype(jnp.float32)
        for d in range(1, nh):
            summed += part_recv[d - 1, :, at].astype(jnp.float32)
        gate = gate_v[pl.ds(step, 1), at]
        out_ref[:, at] = (res_v[:, at].astype(jnp.float32) + gate * summed).astype(out_ref.dtype)
    for cp in sends:
        cp.wait_send()


def per_device(ny, nh, query, key, value, residual, out_weight, gate_table, noise_steps, segment_mask, segment_map):
    rows, n_cols = query.shape
    tok = rows * nh
    n_keys = 2 * ny * tok
    bf, f32 = jnp.bfloat16, jnp.float32
    dma = lambda n: pltpu.SemaphoreType.DMA((n,))
    n_p = max(1, n_cols // CHUNK) * nh
    hbm = pl.BlockSpec(memory_space=pl.ANY)
    smem = pl.BlockSpec(memory_space=pltpu.SMEM)
    return pl.pallas_call(
        functools.partial(kernel, ny, nh, rows),
        out_shape=jax.ShapeDtypeStruct(residual.shape, residual.dtype),
        in_specs=[hbm] * 6 + [smem] * 3,
        out_specs=pl.BlockSpec(memory_space=pltpu.VMEM),
        scratch_shapes=[
            pltpu.VMEM((n_keys, 384), bf),
            pltpu.VMEM((NZ, tok, GW), bf),
            pltpu.VMEM((2, tok, n_keys), f32),
            pltpu.VMEM((tok, 128), f32),
            pltpu.VMEM((tok, 128), f32),
            pltpu.VMEM((tok, 256), f32),
            pltpu.VMEM((tok, 128), f32),
            pltpu.VMEM((NZ - 1, 8, tok), f32),
            pltpu.VMEM((NZ, 8, tok), f32),
            pltpu.VMEM((tok, GW), f32),
            pltpu.VMEM((NZ - 1, tok, GW), bf),
            pltpu.VMEM((NZ - 1, tok, GW), bf),
            pltpu.VMEM((tok, GW), bf),
            pltpu.VMEM(out_weight.shape, bf),
            pltpu.VMEM(gate_table.shape, f32),
            pltpu.VMEM(residual.shape, bf),
            pltpu.VMEM((tok, n_cols), bf),
            pltpu.VMEM((nh - 1, rows, n_cols), bf),
            pltpu.SMEM((NZ * 2 * ny,), f32),
            dma(nh), dma(nh), dma(nh), dma(nh), dma(NZ * nh), dma(NZ * nh),
            dma(ny), dma(ny), dma(ny), dma(ny), dma(ny), dma(ny),
            dma(NZ), dma(NZ), dma(NZ), dma(NZ), dma(n_p), dma(n_p), dma(6),
        ],
        compiler_params=pltpu.CompilerParams(
            collective_id=0, has_side_effects=True, vmem_limit_bytes=56 * 2**20
        ),
        name="segment_attention",
    )(query, key, value, residual, out_weight, gate_table, noise_steps, segment_mask, segment_map)


def solution(mesh):
    nh = mesh.shape["head"]
    ny = mesh.shape["seq"] // (NZ * NC)
    rows = P(("seq", "head"), None)
    return jax.shard_map(
        functools.partial(per_device, ny, nh),
        mesh=mesh,
        in_specs=(rows, rows, rows, rows, P("head", None), P(), P(), P(), P()),
        out_specs=rows,
        check_vma=False,
    )
```

```python
import functools

import jax
import jax.numpy as jnp
from jax import lax
from jax.experimental import pallas as pl
from jax.experimental.pallas import tpu as pltpu
from jax.sharding import PartitionSpec as P

HEAD_DIM = 128
GROUP = 3
GW = GROUP * HEAD_DIM
NZ = 4
NC = 2
NL = 2
HALVES = 2
MASKED = -1e30
FLOOR = -1e20
SCALE = 1.4426950408889634 / HEAD_DIM**0.5
MESH = pl.DeviceIdType.MESH
CHUNK = 1024


def nt_dot(a, b):
    return lax.dot_general(a, b, (((1,), (1,)), ((), ())), preferred_element_type=jnp.float32)


def kernel(
    ny, nh, rows,
    q_hbm, k_hbm, v_hbm, res_hbm, w_hbm, gate_hbm, steps_ref, mask_ref, map_ref,
    out_ref,
    kv, q_all, q_tile, scores, mx_acc, mx, acc, stat_send, stat_recv, o_own, o_send, o_recv,
    attended, w_v, gate_v, res_v, part, x_recv, summed, z_send, z_recv, bias,
    k_ss, k_rs, v_ss, v_rs, q_ss, q_rs, z_ss, z_rs, right_ss, right_rs, left_ss, left_rs,
    sib_ss, sib_rs, o_ss, o_rs, st_ss, st_rs, p_ss, p_rs, e_ss, e_rs, loc,
):
    seq = lax.axis_index("seq")
    head = lax.axis_index("head")
    core = lax.rem(seq, NC)
    zh = lax.rem(seq // NC, NZ)
    y = seq // (NC * NZ)
    nx = nh // NL
    x = head // NL
    zl = lax.rem(head, NL)
    tok = rows * nh
    part_rows = rows // HALVES
    tok_h = tok // HALVES
    n_slots = 2 * ny

    def place(py, pz, pc):
        return (py * NZ + pz) * NC + pc

    def at_head(d):
        return lax.rem(head + d, nh)

    def at_x(d):
        return lax.rem(x + d, nx)

    def at_z(d):
        return lax.rem(zh + d, NZ)

    def at_y(d):
        return lax.rem(y + d + ny, ny)

    def dev(s, h):
        return {"seq": s, "head": h}

    other = place(y, zh, 1 - core)
    right = place(at_y(1), zh, core)
    left = place(at_y(-1), zh, core)
    peers = [dev(seq, at_head(d)) for d in range(1, nh)]
    peers += [dev(place(y, at_z(d), core), head) for d in range(1, NZ)]
    peers += [dev(other, head), dev(right, head), dev(left, head)]

    barrier = pltpu.get_barrier_semaphore()
    for target in peers:
        pl.semaphore_signal(barrier, inc=1, device_id=target, device_id_type=MESH)

    def cols(h, width):
        return pl.ds(pl.multiple_of(h * width, HEAD_DIM), width)

    def own_rows(h, count):
        return pl.ds(pl.multiple_of(h * count, count), count)

    local = [
        pltpu.make_async_copy(k_hbm.at[:, cols(head, HEAD_DIM)], kv.at[own_rows(head, rows), 0:128], loc.at[0]),
        pltpu.make_async_copy(v_hbm.at[:, cols(head, HEAD_DIM)], kv.at[own_rows(head, rows), 128:256], loc.at[1]),
        pltpu.make_async_copy(q_hbm.at[:, :, cols(head, GW)], q_all.at[0, :, own_rows(head, part_rows)], loc.at[2]),
        pltpu.make_async_copy(w_hbm, w_v, loc.at[3]),
        pltpu.make_async_copy(gate_hbm, gate_v, loc.at[4]),
        pltpu.make_async_copy(res_hbm, res_v, loc.at[5]),
    ]
    for cp in local[:3]:
        cp.start()

    q_segs = [map_ref[place(y, at_z(d), core)] for d in range(NZ)]
    for j in range(n_slots):
        k_seg = map_ref[place(at_y(j // 2), zh, core if j % 2 == 0 else 1 - core)]
        for d in range(NZ):
            bias[d * n_slots + j] = jnp.where(mask_ref[q_segs[d], k_seg] > 0, 0.0, MASKED).astype(jnp.float32)

    pl.semaphore_wait(barrier, len(peers))

    sends = []

    def remote(src, dst, ss, rs, target):
        cp = pltpu.make_async_remote_copy(
            src_ref=src, dst_ref=dst, send_sem=ss, recv_sem=rs, device_id=target, device_id_type=MESH
        )
        cp.start()
        sends.append(cp)
        return cp

    kv_in, q_in = [], []
    for d in range(1, nh):
        target = dev(seq, at_head(d))
        kv_in.append(remote(k_hbm.at[:, cols(at_head(d), HEAD_DIM)], kv.at[own_rows(head, rows), 0:128],
                            k_ss.at[d], k_rs.at[d], target))
        kv_in.append(remote(v_hbm.at[:, cols(at_head(d), HEAD_DIM)], kv.at[own_rows(head, rows), 128:256],
                            v_ss.at[d], v_rs.at[d], target))
    for d in range(1, nh):
        q_in.append(remote(q_hbm.at[:, :, cols(at_head(d), GW)], q_all.at[0, :, own_rows(head, part_rows)],
                           q_ss.at[d], q_rs.at[d], dev(seq, at_head(d))))

    z_in = {}

    def send_queries():
        local[2].wait()
        for cp in q_in:
            cp.wait_recv()
        for hf in range(HALVES):
            for dz in (1, 3, 2):
                slot = NZ - dz
                i = hf * NZ + dz
                z_in[hf, slot] = remote(q_all.at[0, hf], q_all.at[slot, hf], z_ss.at[i], z_rs.at[i],
                                        dev(place(y, at_z(dz), core), head))
        for cp in local[3:]:
            cp.start()

    local[0].wait()
    local[1].wait()
    for cp in kv_in:
        cp.wait_recv()

    def block(r, c, lo=0, hi=256):
        return kv.at[pl.ds((r * 2 + c) * tok, tok), lo:hi]

    def ones(i, carry):
        kv[pl.ds(pl.multiple_of(i * 256, 256), 256), 256:384] = jnp.ones((256, 128), jnp.bfloat16)
        return carry

    half = ny // 2
    sib = []
    parts = ((0, 128), (128, 256))

    def pass_on(r, i):
        lo, hi = parts[i]
        sib.append(remote(block(r, 0, lo, hi), block(r, 1, lo, hi),
                          sib_ss.at[2 * r + i], sib_rs.at[2 * r + i], dev(other, head)))

    r_in, l_in = {}, {}
    for s in range(half + 1):
        for i in range(2):
            lo, hi = parts[i]
            if s and i in r_in:
                r_in.pop(i).wait_recv()
            if s < half - 1 or (s == half - 1 and i == 0):
                r_in[i] = remote(block((ny - s) % ny, 0, lo, hi), block((ny - s - 1) % ny, 0, lo, hi),
                                 right_ss.at[2 * s + i], right_rs.at[2 * s + i], dev(right, head))
            if s and i in l_in:
                l_in.pop(i).wait_recv()
            if s < half - 1 or (s == half - 1 and i == 1):
                l_in[i] = remote(block(s, 0, lo, hi), block(s + 1, 0, lo, hi),
                                 left_ss.at[2 * s + i], left_rs.at[2 * s + i], dev(left, head))
            pass_on(s, i)
            if 0 < s < half:
                pass_on(ny - s, i)
        if s == 0:
            send_queries()
            lax.fori_loop(0, n_slots * tok // 256, ones, 0)
    for cp in sib:
        cp.wait_recv()

    n_chunks = n_slots * tok // CHUNK
    per = CHUNK // tok
    rows_t = GROUP * tok_h

    def key_rows_of(jc):
        return pl.ds(pl.multiple_of(jc * CHUNK, CHUNK), CHUNK)

    def first(jc, d, buf):
        s = nt_dot(q_tile[buf], kv[key_rows_of(jc), 0:128])
        scores[buf, :, key_rows_of(jc)] = s
        m = mx_acc[...]
        for b in range(per):
            off = bias[d * n_slots + jc * per + b]
            for e in range(tok // 128):
                at = b * tok + e * 128
                m = jnp.maximum(m, s[:, at:at + 128] + off)
        mx_acc[...] = m

    def second(jc, d, buf):
        m = mx[...]
        pieces = []
        s = scores[buf, :, key_rows_of(jc)]
        for b in range(per):
            shift = (bias[d * n_slots + jc * per + b] - m) * SCALE
            for e in range(tok // 128):
                at = b * tok + e * 128
                pieces.append(jnp.exp2(s[:, at:at + 128] * SCALE + shift).astype(jnp.bfloat16))
        p = jnp.concatenate(pieces, axis=1)
        acc[...] += jnp.dot(p, kv[key_rows_of(jc), 128:384], preferred_element_type=jnp.float32)

    def close_first():
        mx[...] = jnp.broadcast_to(jnp.max(mx_acc[...], axis=1, keepdims=True), (rows_t, 128))
        mx_acc[...] = jnp.full((rows_t, 128), FLOOR, jnp.float32)
        acc[...] = jnp.zeros((rows_t, 256), jnp.float32)

    tiles = [(0, d) for d in (0, 1, 3, 2)] + [(1, d) for d in (1, 3, 2, 0)]
    lane = lax.broadcasted_iota(jnp.int32, (tok_h, 128), 1)

    mx_acc[...] = jnp.full((rows_t, 128), FLOOR, jnp.float32)

    def load_tile(t):
        hf, d = tiles[t]
        if d:
            z_in[hf, d].wait_recv()
        for g in range(GROUP):
            q_tile[t % 2, g * tok_h:(g + 1) * tok_h] = q_all[d, hf, :, g * 128:(g + 1) * 128]

    n_cols = w_v.shape[1]
    o_in, p_in, e_in = {}, {}, {}

    def close_second(hf, d):
        total = jnp.maximum(acc[:, 128:256], 1e-30)
        value = acc[:, 0:128] / total
        level = mx[...] * SCALE + jnp.log2(total)
        stat = level[0:tok_h]
        for g in range(1, GROUP):
            stat = jnp.where(lane == g, level[g * tok_h:(g + 1) * tok_h], stat)
        stat = jnp.transpose(stat)[0:8]
        for g in range(GROUP):
            piece = value[g * tok_h:(g + 1) * tok_h]
            if d == 0:
                o_own[hf, :, g * 128:(g + 1) * 128] = piece
            else:
                o_send[hf, d - 1, :, g * 128:(g + 1) * 128] = piece.astype(jnp.bfloat16)
        if d == 0:
            stat_recv[hf, 0] = stat
            return
        slot = NZ - d
        stat_send[hf, d - 1] = stat
        target = dev(place(y, at_z(d), core), head)
        i = hf * NZ + d
        o_in[hf, slot] = (
            remote(o_send.at[hf, d - 1], o_recv.at[hf, slot - 1], o_ss.at[i], o_rs.at[i], target),
            remote(stat_send.at[hf, d - 1], stat_recv.at[hf, slot], st_ss.at[i], st_rs.at[i], target),
        )

    def project(hf):
        for slot in range(1, NZ):
            for cp in o_in[hf, slot]:
                cp.wait_recv()
        zeros = jnp.zeros((120, tok_h), jnp.float32)
        levels = [jnp.transpose(jnp.concatenate([stat_recv[hf, i], zeros], axis=0)) for i in range(NZ)]
        top = functools.reduce(jnp.maximum, levels)
        shares = [jnp.exp2(v - top) for v in levels]
        whole = functools.reduce(jnp.add, shares)
        shares = [v / whole for v in shares]
        for g in range(GROUP):
            at = slice(g * 128, (g + 1) * 128)
            mixed = shares[0][:, g:g + 1] * o_own[hf, :, at]
            for i in range(1, NZ):
                mixed += shares[i][:, g:g + 1] * o_recv[hf, i - 1, :, at].astype(jnp.float32)
            attended[hf, :, at] = mixed.astype(jnp.bfloat16)
        for ci in range(n_cols // CHUNK):
            at = slice(ci * CHUNK, (ci + 1) * CHUNK)
            part[hf, :, at] = jnp.dot(
                attended[hf], w_v[:, at], preferred_element_type=jnp.float32
            ).astype(jnp.bfloat16)
            for d in range(1, nx):
                i = (hf * (n_cols // CHUNK) + ci) * nx + d
                p_in[hf, ci, d] = remote(
                    part.at[hf, own_rows(at_x(d), NL * part_rows), at], x_recv.at[hf, d - 1, :, at],
                    p_ss.at[i], p_rs.at[i], dev(seq, at_x(d) * NL + zl))

    def exchange(hf):
        for ci in range(n_cols // CHUNK):
            at = slice(ci * CHUNK, (ci + 1) * CHUNK)
            total = part[hf, own_rows(x, NL * part_rows), at].astype(jnp.float32)
            for d in range(1, nx):
                p_in[hf, ci, d].wait_recv()
                total += x_recv[hf, d - 1, :, at].astype(jnp.float32)
            summed[hf, :, at] = total
            z_send[hf, :, at] = summed[hf, own_rows(1 - zl, part_rows), at].astype(jnp.bfloat16)
            i = hf * (n_cols // CHUNK) + ci
            e_in[hf, ci] = remote(z_send.at[hf, :, at], z_recv.at[hf, :, at], e_ss.at[i], e_rs.at[i],
                                  dev(seq, x * NL + 1 - zl))

    def finish(hf, step):
        here = slice(hf * part_rows, (hf + 1) * part_rows)
        for ci in range(n_cols // CHUNK):
            at = slice(ci * CHUNK, (ci + 1) * CHUNK)
            e_in[hf, ci].wait_recv()
            total = summed[hf, own_rows(zl, part_rows), at] + z_recv[hf, :, at].astype(jnp.float32)
            gate = gate_v[pl.ds(step, 1), at]
            out_ref[here, at] = (res_v[here, at].astype(jnp.float32) + gate * total).astype(out_ref.dtype)

    load_tile(0)

    def only_first(jc, carry):
        first(jc, tiles[0][1], 0)
        return carry

    lax.fori_loop(0, n_chunks, only_first, 0)
    close_first()
    for t, (hf, d) in enumerate(tiles):
        more = t + 1 < len(tiles)
        if more:
            load_tile(t + 1)

        def both(jc, carry):
            second(jc, d, t % 2)
            if more:
                first(jc, tiles[t + 1][1], 1 - t % 2)
            return carry

        lax.fori_loop(0, n_chunks, both, 0)
        close_second(hf, d)
        if more:
            close_first()
        if t == len(tiles) - 2:
            local[3].wait()
            project(0)
    project(1)
    exchange(0)
    exchange(1)
    local[4].wait()
    local[5].wait()
    step = steps_ref[map_ref[seq]]
    finish(0, step)
    finish(1, step)
    for cp in sends:
        cp.wait_send()


def per_device(ny, nh, query, key, value, residual, out_weight, gate_table, noise_steps, segment_mask, segment_map):
    rows, n_cols = query.shape
    tok = rows * nh
    half_rows, tok_h = rows // HALVES, tok // HALVES
    rows_t = GROUP * tok_h
    n_keys = 2 * ny * tok
    bf, f32 = jnp.bfloat16, jnp.float32
    dma = lambda n: pltpu.SemaphoreType.DMA((n,))
    n_p = n_cols // CHUNK * HALVES
    nx = nh // NL
    hbm = pl.BlockSpec(memory_space=pl.ANY)
    smem = pl.BlockSpec(memory_space=pltpu.SMEM)
    ring = [dma(2 * ny)] * 6
    return pl.pallas_call(
        functools.partial(kernel, ny, nh, rows),
        out_shape=jax.ShapeDtypeStruct(residual.shape, residual.dtype),
        in_specs=[hbm] * 6 + [smem] * 3,
        out_specs=pl.BlockSpec(memory_space=pltpu.VMEM),
        scratch_shapes=[
            pltpu.VMEM((n_keys, 384), bf),
            pltpu.VMEM((NZ, HALVES, tok_h, GW), bf),
            pltpu.VMEM((2, rows_t, 128), bf),
            pltpu.VMEM((2, rows_t, n_keys), f32),
            pltpu.VMEM((rows_t, 128), f32),
            pltpu.VMEM((rows_t, 128), f32),
            pltpu.VMEM((rows_t, 256), f32),
            pltpu.VMEM((HALVES, NZ - 1, 8, tok_h), f32),
            pltpu.VMEM((HALVES, NZ, 8, tok_h), f32),
            pltpu.VMEM((HALVES, tok_h, GW), f32),
            pltpu.VMEM((HALVES, NZ - 1, tok_h, GW), bf),
            pltpu.VMEM((HALVES, NZ - 1, tok_h, GW), bf),
            pltpu.VMEM((HALVES, tok_h, GW), bf),
            pltpu.VMEM(out_weight.shape, bf),
            pltpu.VMEM(gate_table.shape, f32),
            pltpu.VMEM(residual.shape, bf),
            pltpu.VMEM((HALVES, tok_h, n_cols), bf),
            pltpu.VMEM((HALVES, nx - 1, NL * half_rows, n_cols), bf),
            pltpu.VMEM((HALVES, NL * half_rows, n_cols), f32),
            pltpu.VMEM((HALVES, half_rows, n_cols), bf),
            pltpu.VMEM((HALVES, half_rows, n_cols), bf),
            pltpu.SMEM((NZ * 2 * ny,), f32),
            dma(nh), dma(nh), dma(nh), dma(nh), dma(nh), dma(nh), dma(HALVES * NZ), dma(HALVES * NZ),
            *ring,
            dma(HALVES * NZ), dma(HALVES * NZ), dma(HALVES * NZ), dma(HALVES * NZ),
            dma(n_p * nx), dma(n_p * nx), dma(n_p), dma(n_p), dma(6),
        ],
        compiler_params=pltpu.CompilerParams(
            collective_id=0, has_side_effects=True, vmem_limit_bytes=56 * 2**20
        ),
        name="segment_attention",
    )(
        query.reshape(HALVES, half_rows, n_cols), key, value, residual, out_weight, gate_table,
        noise_steps, segment_mask, segment_map,
    )


def solution(mesh):
    nh = mesh.shape["head"]
    ny = mesh.shape["seq"] // (NZ * NC)
    rows = P(("seq", "head"), None)
    return jax.shard_map(
        functools.partial(per_device, ny, nh),
        mesh=mesh,
        in_specs=(rows, rows, rows, rows, P("head", None), P(), P(), P(), P()),
        out_specs=rows,
        check_vma=False,
    )
```

```python
import functools

import jax
import jax.numpy as jnp
from jax import lax
from jax.experimental import pallas as pl
from jax.experimental.pallas import tpu as pltpu
from jax.sharding import PartitionSpec as P

HEAD_DIM = 128
GROUP = 3
GW = GROUP * HEAD_DIM
NZ = 4
NC = 2
NL = 2
Z_FIRST = ((1, 1), (1, 2))
AHEAD = 3
HALVES = 2
MASKED = -1e30
FLOOR = -1e20
SCALE = 1.4426950408889634 / HEAD_DIM**0.5
MESH = pl.DeviceIdType.MESH
CHUNK = 1024


def nt_dot(a, b):
    return lax.dot_general(a, b, (((1,), (1,)), ((), ())), preferred_element_type=jnp.float32)


def kernel(
    ny, nh, rows,
    q_hbm, k_hbm, v_hbm, res_hbm, w_hbm, gate_hbm, steps_ref, mask_ref, map_ref,
    out_ref,
    keys, values, q_all, q_tile, scores, mx_acc, mx, acc, stat_send, stat_recv, o_own, o_send, o_recv,
    attended, w_v, gate_v, res_v, part, x_recv, summed, z_send, z_recv, zf_recv, xs_send, xs_recv, bias,
    k_ss, k_rs, v_ss, v_rs, q_ss, q_rs, z_ss, z_rs, right_ss, right_rs, left_ss, left_rs,
    sib_ss, sib_rs, o_ss, o_rs, st_ss, st_rs, p_ss, p_rs, e_ss, e_rs, loc,
):
    seq = lax.axis_index("seq")
    head = lax.axis_index("head")
    core = lax.rem(seq, NC)
    zh = lax.rem(seq // NC, NZ)
    y = seq // (NC * NZ)
    nx = nh // NL
    x = head // NL
    zl = lax.rem(head, NL)
    tok = rows * nh
    part_rows = rows // HALVES
    tok_h = tok // HALVES
    n_slots = 2 * ny
    half = ny // 2
    near = [0, 1] + [r for s in range(1, half) for r in (ny - s, s + 1)]
    spot = {r: i for i, r in enumerate(near)}

    def place(py, pz, pc):
        return (py * NZ + pz) * NC + pc

    def at_head(d):
        return lax.rem(head + d, nh)

    def at_x(d):
        return lax.rem(x + d, nx)

    def at_z(d):
        return lax.rem(zh + d, NZ)

    def at_y(d):
        return lax.rem(y + d + ny, ny)

    def dev(s, h):
        return {"seq": s, "head": h}

    other = place(y, zh, 1 - core)
    right = place(at_y(1), zh, core)
    left = place(at_y(-1), zh, core)
    peers = [dev(seq, at_head(d)) for d in range(1, nh)]
    peers += [dev(place(y, at_z(d), core), head) for d in range(1, NZ)]
    peers += [dev(other, head), dev(right, head), dev(left, head)]

    barrier = pltpu.get_barrier_semaphore()
    for target in peers:
        pl.semaphore_signal(barrier, inc=1, device_id=target, device_id_type=MESH)

    def cols(h, width):
        return pl.ds(pl.multiple_of(h * width, HEAD_DIM), width)

    def own_rows(h, count):
        return pl.ds(pl.multiple_of(h * count, count), count)

    local = [
        pltpu.make_async_copy(k_hbm.at[:, cols(head, HEAD_DIM)], keys.at[own_rows(head, rows)], loc.at[0]),
        pltpu.make_async_copy(v_hbm.at[:, cols(head, HEAD_DIM)], values.at[own_rows(head, rows)], loc.at[1]),
        pltpu.make_async_copy(q_hbm.at[:, :, cols(head, GW)], q_all.at[0, :, own_rows(head, part_rows)], loc.at[2]),
        pltpu.make_async_copy(w_hbm, w_v, loc.at[3]),
        pltpu.make_async_copy(gate_hbm, gate_v, loc.at[4]),
        pltpu.make_async_copy(res_hbm, res_v, loc.at[5]),
    ]
    for cp in local[:3]:
        cp.start()

    q_segs = [map_ref[place(y, at_z(d), core)] for d in range(NZ)]
    for j in range(n_slots):
        k_seg = map_ref[place(at_y(near[j // 2]), zh, core if j % 2 == 0 else 1 - core)]
        for d in range(NZ):
            bias[d * n_slots + j] = jnp.where(mask_ref[q_segs[d], k_seg] > 0, 0.0, MASKED).astype(jnp.float32)

    pl.semaphore_wait(barrier, len(peers))

    sends = []

    def remote(src, dst, ss, rs, target):
        cp = pltpu.make_async_remote_copy(
            src_ref=src, dst_ref=dst, send_sem=ss, recv_sem=rs, device_id=target, device_id_type=MESH
        )
        cp.start()
        sends.append(cp)
        return cp

    kv_in, q_in = [], []
    for d in range(1, nh):
        target = dev(seq, at_head(d))
        kv_in.append(remote(k_hbm.at[:, cols(at_head(d), HEAD_DIM)], keys.at[own_rows(head, rows)],
                            k_ss.at[d], k_rs.at[d], target))
        kv_in.append(remote(v_hbm.at[:, cols(at_head(d), HEAD_DIM)], values.at[own_rows(head, rows)],
                            v_ss.at[d], v_rs.at[d], target))
    for d in range(1, nh):
        q_in.append(remote(q_hbm.at[:, :, cols(at_head(d), GW)], q_all.at[0, :, own_rows(head, part_rows)],
                           q_ss.at[d], q_rs.at[d], dev(seq, at_head(d))))

    z_in = {}

    def send_queries():
        local[2].wait()
        for cp in q_in:
            cp.wait_recv()
        for hf in range(HALVES):
            for dz in (1, 3, 2):
                slot = NZ - dz
                i = hf * NZ + dz
                z_in[hf, slot] = remote(q_all.at[0, hf], q_all.at[slot, hf], z_ss.at[i], z_rs.at[i],
                                        dev(place(y, at_z(dz), core), head))
        for cp in local[3:]:
            cp.start()

    local[0].wait()
    local[1].wait()
    for cp in kv_in:
        cp.wait_recv()

    def block(r, c, held):
        return held.at[pl.ds((spot[r] * 2 + c) * tok, tok)]

    n_chunks = n_slots * tok // CHUNK
    per = CHUNK // tok
    rows_t = GROUP * tok_h

    def key_rows_of(jc):
        return pl.ds(pl.multiple_of(jc * CHUNK, CHUNK), CHUNK)

    def first(jc, d, buf):
        s = nt_dot(q_tile[buf], keys[key_rows_of(jc)])
        scores[buf, :, key_rows_of(jc)] = s
        m = mx_acc[buf]
        for b in range(per):
            off = bias[d * n_slots + jc * per + b]
            for e in range(tok // 128):
                at = b * tok + e * 128
                m = jnp.maximum(m, s[:, at:at + 128] + off)
        mx_acc[buf] = m

    def second(jc, d, buf):
        m = mx[buf]
        pieces = []
        s = scores[buf, :, key_rows_of(jc)]
        for b in range(per):
            shift = (bias[d * n_slots + jc * per + b] - m) * SCALE
            for e in range(tok // 128):
                at = b * tok + e * 128
                pieces.append(jnp.exp2(s[:, at:at + 128] * SCALE + shift).astype(jnp.bfloat16))
        p = jnp.concatenate(pieces, axis=1)
        beside = jnp.concatenate([values[key_rows_of(jc)], jnp.ones((CHUNK, 128), jnp.bfloat16)], axis=1)
        acc[...] += jnp.dot(p, beside, preferred_element_type=jnp.float32)

    def open_first(buf):
        mx_acc[buf] = jnp.full((rows_t, 128), FLOOR, jnp.float32)

    def close_first(buf):
        mx[buf] = jnp.broadcast_to(jnp.max(mx_acc[buf], axis=1, keepdims=True), (rows_t, 128))

    tiles = [(hf, d) for hf in range(HALVES) for d in (1, 3, 2, 0)]
    lane = lax.broadcasted_iota(jnp.int32, (tok_h, 128), 1)

    def load_tile(t):
        hf, d = tiles[t]
        if d:
            z_in[hf, d].wait_recv()
        for g in range(GROUP):
            q_tile[t % AHEAD, g * tok_h:(g + 1) * tok_h] = q_all[d, hf, :, g * 128:(g + 1) * 128]
        open_first(t % AHEAD)

    def early(lo, hi):
        for t in range(AHEAD - 1):
            def step_early(jc, carry, t=t):
                first(jc, tiles[t][1], t)
                return carry

            lax.fori_loop(lo, hi, step_early, 0)

    sib = {}
    parts = (keys, values)

    def pass_on(r, i):
        sib[r, i] = remote(block(r, 0, parts[i]), block(r, 1, parts[i]),
                           sib_ss.at[2 * r + i], sib_rs.at[2 * r + i], dev(other, head))

    waited = []

    def arrived(count):
        for r in near[:2 * (count - 1)]:
            for i in range(2):
                if (r, i) not in waited:
                    waited.append((r, i))
                    sib[r, i].wait_recv()

    r_in, l_in = {}, {}
    for s in range(half + 1):
        for i in range(2):
            held = parts[i]
            if s and i in r_in:
                r_in.pop(i).wait_recv()
            if s < half - 1 or (s == half - 1 and i == 0):
                r_in[i] = remote(block((ny - s) % ny, 0, held), block((ny - s - 1) % ny, 0, held),
                                 right_ss.at[2 * s + i], right_rs.at[2 * s + i], dev(right, head))
            if s and i in l_in:
                l_in.pop(i).wait_recv()
            if s < half - 1 or (s == half - 1 and i == 1):
                l_in[i] = remote(block(s, 0, held), block(s + 1, 0, held),
                                 left_ss.at[2 * s + i], left_rs.at[2 * s + i], dev(left, head))
            pass_on(s, i)
            if 0 < s < half:
                pass_on(ny - s, i)
        if s == 0:
            send_queries()
        if s == half - 1:
            for t in range(AHEAD - 1):
                load_tile(t)
            arrived(half - 1)
            early(0, half - 2)
    arrived(half)
    early(half - 2, half - 1)
    arrived(half + 1)
    early(half - 1, half)

    n_cols = w_v.shape[1]
    n_p = n_cols // CHUNK
    o_in, p_in, e_in = {}, {}, {}

    def close_second(hf, d, buf):
        total = jnp.maximum(acc[:, 128:256], 1e-30)
        value = acc[:, 0:128] / total
        level = mx[buf] * SCALE + jnp.log2(total)
        stat = level[0:tok_h]
        for g in range(1, GROUP):
            stat = jnp.where(lane == g, level[g * tok_h:(g + 1) * tok_h], stat)
        stat = jnp.transpose(stat)[0:8]
        for g in range(GROUP):
            piece = value[g * tok_h:(g + 1) * tok_h]
            if d == 0:
                o_own[hf, :, g * 128:(g + 1) * 128] = piece
            else:
                o_send[hf, d - 1, :, g * 128:(g + 1) * 128] = piece.astype(jnp.bfloat16)
        if d == 0:
            stat_recv[hf, 0] = stat
            return
        slot = NZ - d
        stat_send[hf, d - 1] = stat
        target = dev(place(y, at_z(d), core), head)
        i = hf * NZ + d
        o_in[hf, slot] = (
            remote(o_send.at[hf, d - 1], o_recv.at[hf, slot - 1], o_ss.at[i], o_rs.at[i], target),
            remote(stat_send.at[hf, d - 1], stat_recv.at[hf, slot], st_ss.at[i], st_rs.at[i], target),
        )

    def project(hf):
        for slot in range(1, NZ):
            for cp in o_in[hf, slot]:
                cp.wait_recv()
        zeros = jnp.zeros((120, tok_h), jnp.float32)
        levels = [jnp.transpose(jnp.concatenate([stat_recv[hf, i], zeros], axis=0)) for i in range(NZ)]
        top = functools.reduce(jnp.maximum, levels)
        shares = [jnp.exp2(v - top) for v in levels]
        whole = functools.reduce(jnp.add, shares)
        shares = [v / whole for v in shares]
        for g in range(GROUP):
            at = slice(g * 128, (g + 1) * 128)
            mixed = shares[0][:, g:g + 1] * o_own[hf, :, at]
            for i in range(1, NZ):
                mixed += shares[i][:, g:g + 1] * o_recv[hf, i - 1, :, at].astype(jnp.float32)
            attended[hf, :, at] = mixed.astype(jnp.bfloat16)
        for ci in (1, 2, 0):
            at = slice(ci * CHUNK, (ci + 1) * CHUNK)
            product = jnp.dot(attended[hf], w_v[:, at], preferred_element_type=jnp.float32)
            part[hf, :, :, :, at] = product.astype(jnp.bfloat16).reshape(nx, NL, part_rows, CHUNK)
            if (hf, ci) in Z_FIRST:
                i = hf * n_p + ci
                e_in[hf, ci] = remote(part.at[hf, :, 1 - zl, :, at], zf_recv.at[:, :, at],
                                      e_ss.at[i], e_rs.at[i], dev(seq, x * NL + 1 - zl))
                continue
            for d in range(1, nx):
                i = (hf * n_p + ci) * nx + d
                p_in[hf, ci, d] = remote(part.at[hf, at_x(d), :, :, at], x_recv.at[hf, d - 1, :, :, at],
                                         p_ss.at[i], p_rs.at[i], dev(seq, at_x(d) * NL + zl))

    def exchange(hf, ci):
        at = slice(ci * CHUNK, (ci + 1) * CHUNK)
        if (hf, ci) in Z_FIRST:
            e_in[hf, ci].wait_recv()
            for d in range(nx):
                total = part[hf, at_x(d), zl, :, at].astype(jnp.float32) + zf_recv[at_x(d), :, at].astype(jnp.float32)
                if d == 0:
                    summed[hf, 0, :, at] = total
                    continue
                xs_send[d - 1, :, at] = total.astype(jnp.bfloat16)
                i = (hf * n_p + ci) * nx + d
                p_in[hf, ci, d] = remote(xs_send.at[d - 1, :, at], xs_recv.at[d - 1, :, at],
                                         p_ss.at[i], p_rs.at[i], dev(seq, at_x(d) * NL + zl))
            return
        total = part[hf, x, :, :, at].astype(jnp.float32)
        for d in range(1, nx):
            p_in[hf, ci, d].wait_recv()
            total += x_recv[hf, d - 1, :, :, at].astype(jnp.float32)
        summed[hf, :, :, at] = total
        z_send[hf, :, at] = summed[hf, 1 - zl, :, at].astype(jnp.bfloat16)
        i = hf * n_p + ci
        e_in[hf, ci] = remote(z_send.at[hf, :, at], z_recv.at[hf, :, at], e_ss.at[i], e_rs.at[i],
                              dev(seq, x * NL + 1 - zl))

    def finish(hf, ci, step):
        here = slice(hf * part_rows, (hf + 1) * part_rows)
        at = slice(ci * CHUNK, (ci + 1) * CHUNK)
        if (hf, ci) in Z_FIRST:
            total = summed[hf, 0, :, at]
            for d in range(1, nx):
                p_in[hf, ci, d].wait_recv()
                total += xs_recv[d - 1, :, at].astype(jnp.float32)
        else:
            e_in[hf, ci].wait_recv()
            total = summed[hf, zl, :, at] + z_recv[hf, :, at].astype(jnp.float32)
        gate = gate_v[pl.ds(step, 1), at]
        out_ref[here, at] = (res_v[here, at].astype(jnp.float32) + gate * total).astype(out_ref.dtype)

    for t in range(AHEAD - 1):
        close_first(t)
    for t, (hf, d) in enumerate(tiles):
        ahead = t + AHEAD - 1
        more = ahead < len(tiles)
        if more:
            load_tile(ahead)
        acc[...] = jnp.zeros((rows_t, 256), jnp.float32)

        def both(jc, carry):
            second(jc, d, t % AHEAD)
            if more:
                first(jc, tiles[ahead][1], ahead % AHEAD)
            return carry

        lax.fori_loop(0, n_chunks, both, 0)
        close_second(hf, d, t % AHEAD)
        if more:
            close_first(ahead % AHEAD)
        if t == len(tiles) - 2:
            local[3].wait()
            project(0)
    project(1)
    later = [(1, ci) for ci in (1, 2, 0)]
    for ci in range(n_p):
        exchange(0, ci)
    for hf, ci in later:
        exchange(hf, ci)
    local[4].wait()
    local[5].wait()
    step = steps_ref[map_ref[seq]]
    for ci in range(n_p):
        finish(0, ci, step)
    for hf, ci in later:
        finish(hf, ci, step)
    for cp in sends:
        cp.wait_send()


def per_device(ny, nh, query, key, value, residual, out_weight, gate_table, noise_steps, segment_mask, segment_map):
    rows, n_cols = query.shape
    tok = rows * nh
    half_rows, tok_h = rows // HALVES, tok // HALVES
    rows_t = GROUP * tok_h
    n_keys = 2 * ny * tok
    bf, f32 = jnp.bfloat16, jnp.float32
    dma = lambda n: pltpu.SemaphoreType.DMA((n,))
    n_p = n_cols // CHUNK * HALVES
    nx = nh // NL
    hbm = pl.BlockSpec(memory_space=pl.ANY)
    smem = pl.BlockSpec(memory_space=pltpu.SMEM)
    ring = [dma(2 * ny)] * 6
    return pl.pallas_call(
        functools.partial(kernel, ny, nh, rows),
        out_shape=jax.ShapeDtypeStruct(residual.shape, residual.dtype),
        in_specs=[hbm] * 6 + [smem] * 3,
        out_specs=pl.BlockSpec(memory_space=pltpu.VMEM),
        scratch_shapes=[
            pltpu.VMEM((n_keys, HEAD_DIM), bf),
            pltpu.VMEM((n_keys, HEAD_DIM), bf),
            pltpu.VMEM((NZ, HALVES, tok_h, GW), bf),
            pltpu.VMEM((AHEAD, rows_t, 128), bf),
            pltpu.VMEM((AHEAD, rows_t, n_keys), f32),
            pltpu.VMEM((AHEAD, rows_t, 128), f32),
            pltpu.VMEM((AHEAD, rows_t, 128), f32),
            pltpu.VMEM((rows_t, 256), f32),
            pltpu.VMEM((HALVES, NZ - 1, 8, tok_h), f32),
            pltpu.VMEM((HALVES, NZ, 8, tok_h), f32),
            pltpu.VMEM((HALVES, tok_h, GW), f32),
            pltpu.VMEM((HALVES, NZ - 1, tok_h, GW), bf),
            pltpu.VMEM((HALVES, NZ - 1, tok_h, GW), bf),
            pltpu.VMEM((HALVES, tok_h, GW), bf),
            pltpu.VMEM(out_weight.shape, bf),
            pltpu.VMEM(gate_table.shape, f32),
            pltpu.VMEM(residual.shape, bf),
            pltpu.VMEM((HALVES, nx, NL, half_rows, n_cols), bf),
            pltpu.VMEM((HALVES, nx - 1, NL, half_rows, n_cols), bf),
            pltpu.VMEM((HALVES, NL, half_rows, n_cols), f32),
            pltpu.VMEM((HALVES, half_rows, n_cols), bf),
            pltpu.VMEM((HALVES, half_rows, n_cols), bf),
            pltpu.VMEM((nx, half_rows, n_cols), bf),
            pltpu.VMEM((nx - 1, half_rows, n_cols), bf),
            pltpu.VMEM((nx - 1, half_rows, n_cols), bf),
            pltpu.SMEM((NZ * 2 * ny,), f32),
            dma(nh), dma(nh), dma(nh), dma(nh), dma(nh), dma(nh), dma(HALVES * NZ), dma(HALVES * NZ),
            *ring,
            dma(HALVES * NZ), dma(HALVES * NZ), dma(HALVES * NZ), dma(HALVES * NZ),
            dma(n_p * nx), dma(n_p * nx), dma(n_p), dma(n_p), dma(6),
        ],
        compiler_params=pltpu.CompilerParams(
            collective_id=0, has_side_effects=True, vmem_limit_bytes=56 * 2**20
        ),
        name="segment_attention",
    )(
        query.reshape(HALVES, half_rows, n_cols), key, value, residual, out_weight, gate_table,
        noise_steps, segment_mask, segment_map,
    )


def solution(mesh):
    nh = mesh.shape["head"]
    ny = mesh.shape["seq"] // (NZ * NC)
    rows = P(("seq", "head"), None)
    return jax.shard_map(
        functools.partial(per_device, ny, nh),
        mesh=mesh,
        in_specs=(rows, rows, rows, rows, P("head", None), P(), P(), P(), P()),
        out_specs=rows,
        check_vma=False,
    )
```

```python
import functools

import jax
import jax.numpy as jnp
from jax import lax
from jax.experimental import pallas as pl
from jax.experimental.pallas import tpu as pltpu
from jax.sharding import PartitionSpec as P

HEAD_DIM = 128
GROUP = 3
GW = GROUP * HEAD_DIM
NZ = 4
NC = 2
NL = 2
Z_FIRST = ((1, 1), (1, 2))
AHEAD = 3
HALVES = 2
MASKED = -1e30
FLOOR = -1e20
SCALE = 1.4426950408889634 / HEAD_DIM**0.5
MESH = pl.DeviceIdType.MESH
CHUNK = 1024


def nt_dot(a, b):
    return lax.dot_general(a, b, (((1,), (1,)), ((), ())), preferred_element_type=jnp.float32)


def kernel(
    ny, nh, rows,
    q_hbm, k_hbm, v_hbm, res_hbm, w_hbm, gate_hbm, steps_ref, mask_ref, map_ref,
    out_ref,
    keys, values, q_all, q_tile, scores, mx_acc, mx, acc, stat_send, stat_recv, o_own, o_send, o_recv,
    attended, w_v, gate_v, res_v, part, x_recv, summed, z_send, z_recv, zf_recv, xs_send, xs_recv, bias,
    k_ss, k_rs, v_ss, v_rs, q_ss, q_rs, z_ss, z_rs, ring_ss, ring_rs,
    sib_ss, sib_rs, o_ss, o_rs, st_ss, st_rs, p_ss, p_rs, e_ss, e_rs, loc,
):
    seq = lax.axis_index("seq")
    head = lax.axis_index("head")
    core = lax.rem(seq, NC)
    zh = lax.rem(seq // NC, NZ)
    y = seq // (NC * NZ)
    nx = nh // NL
    x = head // NL
    zl = lax.rem(head, NL)
    tok = rows * nh
    part_rows = rows // HALVES
    tok_h = tok // HALVES
    n_slots = 2 * ny
    half = ny // 2
    near = [0, 1] + [r for s in range(1, half) for r in (ny - s, s + 1)]
    spot = {r: i for i, r in enumerate(near)}

    def place(py, pz, pc):
        return (py * NZ + pz) * NC + pc

    def at_head(d):
        return lax.rem(head + d, nh)

    def at_x(d):
        return lax.rem(x + d, nx)

    def at_z(d):
        return lax.rem(zh + d, NZ)

    def at_y(d):
        return lax.rem(y + d + ny, ny)

    def dev(s, h):
        return {"seq": s, "head": h}

    other = place(y, zh, 1 - core)
    right = place(at_y(1), zh, core)
    left = place(at_y(-1), zh, core)
    peers = [dev(seq, at_head(d)) for d in range(1, nh)]
    peers += [dev(place(y, at_z(d), core), head) for d in range(1, NZ)]
    right2, left2 = place(at_y(2), zh, core), place(at_y(-2), zh, core)
    peers += [dev(other, head)] + [dev(p, head) for p in (right, left, right2, left2)]

    barrier = pltpu.get_barrier_semaphore()
    for target in peers:
        pl.semaphore_signal(barrier, inc=1, device_id=target, device_id_type=MESH)

    def cols(h, width):
        return pl.ds(pl.multiple_of(h * width, HEAD_DIM), width)

    def own_rows(h, count):
        return pl.ds(pl.multiple_of(h * count, count), count)

    local = [
        pltpu.make_async_copy(k_hbm.at[:, cols(head, HEAD_DIM)], keys.at[own_rows(head, rows)], loc.at[0]),
        pltpu.make_async_copy(v_hbm.at[:, cols(head, HEAD_DIM)], values.at[own_rows(head, rows)], loc.at[1]),
        pltpu.make_async_copy(q_hbm.at[:, :, cols(head, GW)], q_all.at[0, :, own_rows(head, part_rows)], loc.at[2]),
        pltpu.make_async_copy(w_hbm, w_v, loc.at[3]),
        pltpu.make_async_copy(gate_hbm, gate_v, loc.at[4]),
        pltpu.make_async_copy(res_hbm, res_v, loc.at[5]),
    ]
    for cp in local[:3]:
        cp.start()

    q_segs = [map_ref[place(y, at_z(d), core)] for d in range(NZ)]
    for j in range(n_slots):
        k_seg = map_ref[place(at_y(near[j // 2]), zh, core if j % 2 == 0 else 1 - core)]
        for d in range(NZ):
            bias[d * n_slots + j] = jnp.where(mask_ref[q_segs[d], k_seg] > 0, 0.0, MASKED).astype(jnp.float32)

    pl.semaphore_wait(barrier, len(peers))

    sends = []

    def remote(src, dst, ss, rs, target):
        cp = pltpu.make_async_remote_copy(
            src_ref=src, dst_ref=dst, send_sem=ss, recv_sem=rs, device_id=target, device_id_type=MESH
        )
        cp.start()
        sends.append(cp)
        return cp

    kv_in, q_in = [], []
    for d in range(1, nh):
        target = dev(seq, at_head(d))
        kv_in.append(remote(k_hbm.at[:, cols(at_head(d), HEAD_DIM)], keys.at[own_rows(head, rows)],
                            k_ss.at[d], k_rs.at[d], target))
        kv_in.append(remote(v_hbm.at[:, cols(at_head(d), HEAD_DIM)], values.at[own_rows(head, rows)],
                            v_ss.at[d], v_rs.at[d], target))
    for d in range(1, nh):
        q_in.append(remote(q_hbm.at[:, :, cols(at_head(d), GW)], q_all.at[0, :, own_rows(head, part_rows)],
                           q_ss.at[d], q_rs.at[d], dev(seq, at_head(d))))

    z_in = {}

    def send_queries():
        local[2].wait()
        for cp in q_in:
            cp.wait_recv()
        for hf in range(HALVES):
            for dz in (1, 3, 2):
                slot = NZ - dz
                i = hf * NZ + dz
                z_in[hf, slot] = remote(q_all.at[0, hf], q_all.at[slot, hf], z_ss.at[i], z_rs.at[i],
                                        dev(place(y, at_z(dz), core), head))
        for cp in local[3:]:
            cp.start()

    local[0].wait()
    local[1].wait()
    for cp in kv_in:
        cp.wait_recv()

    def block(r, c, held):
        return held.at[pl.ds((spot[r] * 2 + c) * tok, tok)]

    n_chunks = n_slots * tok // CHUNK
    per = CHUNK // tok
    rows_t = GROUP * tok_h

    def key_rows_of(jc):
        return pl.ds(pl.multiple_of(jc * CHUNK, CHUNK), CHUNK)

    def first(jc, d, buf):
        s = nt_dot(q_tile[buf], keys[key_rows_of(jc)])
        scores[buf, :, key_rows_of(jc)] = s
        m = mx_acc[buf]
        for b in range(per):
            off = bias[d * n_slots + jc * per + b]
            for e in range(tok // 128):
                at = b * tok + e * 128
                m = jnp.maximum(m, s[:, at:at + 128] + off)
        mx_acc[buf] = m

    def second(jc, d, buf):
        m = mx[buf]
        pieces = []
        s = scores[buf, :, key_rows_of(jc)]
        for b in range(per):
            shift = (bias[d * n_slots + jc * per + b] - m) * SCALE
            for e in range(tok // 128):
                at = b * tok + e * 128
                pieces.append(jnp.exp2(s[:, at:at + 128] * SCALE + shift).astype(jnp.bfloat16))
        p = jnp.concatenate(pieces, axis=1)
        beside = jnp.concatenate([values[key_rows_of(jc)], jnp.ones((CHUNK, 128), jnp.bfloat16)], axis=1)
        acc[...] += jnp.dot(p, beside, preferred_element_type=jnp.float32)

    def open_first(buf):
        mx_acc[buf] = jnp.full((rows_t, 128), FLOOR, jnp.float32)

    def close_first(buf):
        mx[buf] = jnp.broadcast_to(jnp.max(mx_acc[buf], axis=1, keepdims=True), (rows_t, 128))

    tiles = [(hf, d) for hf in range(HALVES) for d in (1, 3, 2)] + [(hf, 0) for hf in range(HALVES)]
    lane = lax.broadcasted_iota(jnp.int32, (tok_h, 128), 1)

    def load_tile(t):
        hf, d = tiles[t]
        if d:
            z_in[hf, d].wait_recv()
        for g in range(GROUP):
            q_tile[t % AHEAD, g * tok_h:(g + 1) * tok_h] = q_all[d, hf, :, g * 128:(g + 1) * 128]
        open_first(t % AHEAD)

    def early(lo, hi):
        for t in range(AHEAD - 1):
            def step_early(jc, carry, t=t):
                first(jc, tiles[t][1], t)
                return carry

            lax.fori_loop(lo, hi, step_early, 0)

    sib = {}
    parts = (keys, values)

    def pass_on(r, i):
        sib[r, i] = remote(block(r, 0, parts[i]), block(r, 1, parts[i]),
                           sib_ss.at[2 * r + i], sib_rs.at[2 * r + i], dev(other, head))

    waited = []

    def arrived(count):
        for r in near[:2 * (count - 1)]:
            for i in range(2):
                if (r, i) not in waited:
                    waited.append((r, i))
                    sib[r, i].wait_recv()

    ring = {}

    def go(r, i, d):
        to = {1: right, -1: left, 2: right2, -2: left2}[d]
        at = (r - d) % ny
        ring[at, i] = remote(block(r, 0, parts[i]), block(at, 0, parts[i]),
                             ring_ss.at[2 * at + i], ring_rs.at[2 * at + i], dev(to, head))

    for i in range(2):
        for d in (2, -2):
            go(0, i, d)
    for i in range(2):
        for d in (1, -1):
            go(0, i, d)
    send_queries()
    for i in range(2):
        pass_on(0, i)
    for i in range(2):
        for d in (2, -2):
            r = -d % ny
            ring[r, i].wait_recv()
            go(r, i, d // 2)
            if (i == 0) == (d > 0):
                go(r, i, d)
    for r in (ny - 2, 2, 1, ny - 1):
        for i in range(2):
            if r in (1, ny - 1):
                ring[r, i].wait_recv()
            pass_on(r, i)
    for t in range(AHEAD - 1):
        load_tile(t)
    arrived(half - 1)
    early(0, half - 2)
    for r in (ny - 3, 3, half):
        for i in range(2):
            ring[r, i].wait_recv()
            pass_on(r, i)
    arrived(half)
    early(half - 2, half - 1)
    arrived(half + 1)
    early(half - 1, half)

    n_cols = w_v.shape[1]
    n_p = n_cols // CHUNK
    o_in, p_in, e_in = {}, {}, {}

    def close_second(hf, d, buf):
        total = jnp.maximum(acc[:, 128:256], 1e-30)
        value = acc[:, 0:128] / total
        level = mx[buf] * SCALE + jnp.log2(total)
        stat = level[0:tok_h]
        for g in range(1, GROUP):
            stat = jnp.where(lane == g, level[g * tok_h:(g + 1) * tok_h], stat)
        stat = jnp.transpose(stat)[0:8]
        for g in range(GROUP):
            piece = value[g * tok_h:(g + 1) * tok_h]
            if d == 0:
                o_own[hf, :, g * 128:(g + 1) * 128] = piece
            else:
                o_send[hf, d - 1, :, g * 128:(g + 1) * 128] = piece.astype(jnp.bfloat16)
        if d == 0:
            stat_recv[hf, 0] = stat
            return
        slot = NZ - d
        stat_send[hf, d - 1] = stat
        target = dev(place(y, at_z(d), core), head)
        i = hf * NZ + d
        o_in[hf, slot] = (
            remote(o_send.at[hf, d - 1], o_recv.at[hf, slot - 1], o_ss.at[i], o_rs.at[i], target),
            remote(stat_send.at[hf, d - 1], stat_recv.at[hf, slot], st_ss.at[i], st_rs.at[i], target),
        )

    def project(hf):
        for slot in range(1, NZ):
            for cp in o_in[hf, slot]:
                cp.wait_recv()
        zeros = jnp.zeros((120, tok_h), jnp.float32)
        levels = [jnp.transpose(jnp.concatenate([stat_recv[hf, i], zeros], axis=0)) for i in range(NZ)]
        top = functools.reduce(jnp.maximum, levels)
        shares = [jnp.exp2(v - top) for v in levels]
        whole = functools.reduce(jnp.add, shares)
        shares = [v / whole for v in shares]
        for g in range(GROUP):
            at = slice(g * 128, (g + 1) * 128)
            mixed = shares[0][:, g:g + 1] * o_own[hf, :, at]
            for i in range(1, NZ):
                mixed += shares[i][:, g:g + 1] * o_recv[hf, i - 1, :, at].astype(jnp.float32)
            attended[hf, :, at] = mixed.astype(jnp.bfloat16)
        for ci in (1, 2, 0):
            at = slice(ci * CHUNK, (ci + 1) * CHUNK)
            product = jnp.dot(attended[hf], w_v[:, at], preferred_element_type=jnp.float32)
            part[hf, :, :, :, at] = product.astype(jnp.bfloat16).reshape(nx, NL, part_rows, CHUNK)
            if (hf, ci) in Z_FIRST:
                i = hf * n_p + ci
                e_in[hf, ci] = remote(part.at[hf, :, 1 - zl, :, at], zf_recv.at[:, :, at],
                                      e_ss.at[i], e_rs.at[i], dev(seq, x * NL + 1 - zl))
                continue
            for d in range(1, nx):
                i = (hf * n_p + ci) * nx + d
                p_in[hf, ci, d] = remote(part.at[hf, at_x(d), :, :, at], x_recv.at[hf, d - 1, :, :, at],
                                         p_ss.at[i], p_rs.at[i], dev(seq, at_x(d) * NL + zl))

    def exchange(hf, ci):
        at = slice(ci * CHUNK, (ci + 1) * CHUNK)
        if (hf, ci) in Z_FIRST:
            e_in[hf, ci].wait_recv()
            for d in range(nx):
                total = part[hf, at_x(d), zl, :, at].astype(jnp.float32) + zf_recv[at_x(d), :, at].astype(jnp.float32)
                if d == 0:
                    summed[hf, 0, :, at] = total
                    continue
                xs_send[d - 1, :, at] = total.astype(jnp.bfloat16)
                i = (hf * n_p + ci) * nx + d
                p_in[hf, ci, d] = remote(xs_send.at[d - 1, :, at], xs_recv.at[d - 1, :, at],
                                         p_ss.at[i], p_rs.at[i], dev(seq, at_x(d) * NL + zl))
            return
        total = part[hf, x, :, :, at].astype(jnp.float32)
        for d in range(1, nx):
            p_in[hf, ci, d].wait_recv()
            total += x_recv[hf, d - 1, :, :, at].astype(jnp.float32)
        summed[hf, :, :, at] = total
        z_send[hf, :, at] = summed[hf, 1 - zl, :, at].astype(jnp.bfloat16)
        i = hf * n_p + ci
        e_in[hf, ci] = remote(z_send.at[hf, :, at], z_recv.at[hf, :, at], e_ss.at[i], e_rs.at[i],
                              dev(seq, x * NL + 1 - zl))

    def finish(hf, ci, step):
        here = slice(hf * part_rows, (hf + 1) * part_rows)
        at = slice(ci * CHUNK, (ci + 1) * CHUNK)
        if (hf, ci) in Z_FIRST:
            total = summed[hf, 0, :, at]
            for d in range(1, nx):
                p_in[hf, ci, d].wait_recv()
                total += xs_recv[d - 1, :, at].astype(jnp.float32)
        else:
            e_in[hf, ci].wait_recv()
            total = summed[hf, zl, :, at] + z_recv[hf, :, at].astype(jnp.float32)
        gate = gate_v[pl.ds(step, 1), at]
        out_ref[here, at] = (res_v[here, at].astype(jnp.float32) + gate * total).astype(out_ref.dtype)

    for t in range(AHEAD - 1):
        close_first(t)
    for t, (hf, d) in enumerate(tiles):
        ahead = t + AHEAD - 1
        more = ahead < len(tiles)
        if more:
            load_tile(ahead)
        acc[...] = jnp.zeros((rows_t, 256), jnp.float32)

        def both(jc, carry):
            second(jc, d, t % AHEAD)
            if more:
                first(jc, tiles[ahead][1], ahead % AHEAD)
            return carry

        lax.fori_loop(0, n_chunks, both, 0)
        close_second(hf, d, t % AHEAD)
        if more:
            close_first(ahead % AHEAD)
        if t == len(tiles) - 2:
            local[3].wait()
            project(0)
    project(1)
    later = [(1, ci) for ci in (1, 2, 0)]
    for ci in range(n_p):
        exchange(0, ci)
    for hf, ci in later:
        exchange(hf, ci)
    local[4].wait()
    local[5].wait()
    step = steps_ref[map_ref[seq]]
    for ci in range(n_p):
        finish(0, ci, step)
    for hf, ci in later:
        finish(hf, ci, step)
    for cp in sends:
        cp.wait_send()


def per_device(ny, nh, query, key, value, residual, out_weight, gate_table, noise_steps, segment_mask, segment_map):
    rows, n_cols = query.shape
    tok = rows * nh
    half_rows, tok_h = rows // HALVES, tok // HALVES
    rows_t = GROUP * tok_h
    n_keys = 2 * ny * tok
    bf, f32 = jnp.bfloat16, jnp.float32
    dma = lambda n: pltpu.SemaphoreType.DMA((n,))
    n_p = n_cols // CHUNK * HALVES
    nx = nh // NL
    hbm = pl.BlockSpec(memory_space=pl.ANY)
    smem = pl.BlockSpec(memory_space=pltpu.SMEM)
    ring = [dma(2 * ny)] * 4
    return pl.pallas_call(
        functools.partial(kernel, ny, nh, rows),
        out_shape=jax.ShapeDtypeStruct(residual.shape, residual.dtype),
        in_specs=[hbm] * 6 + [smem] * 3,
        out_specs=pl.BlockSpec(memory_space=pltpu.VMEM),
        scratch_shapes=[
            pltpu.VMEM((n_keys, HEAD_DIM), bf),
            pltpu.VMEM((n_keys, HEAD_DIM), bf),
            pltpu.VMEM((NZ, HALVES, tok_h, GW), bf),
            pltpu.VMEM((AHEAD, rows_t, 128), bf),
            pltpu.VMEM((AHEAD, rows_t, n_keys), f32),
            pltpu.VMEM((AHEAD, rows_t, 128), f32),
            pltpu.VMEM((AHEAD, rows_t, 128), f32),
            pltpu.VMEM((rows_t, 256), f32),
            pltpu.VMEM((HALVES, NZ - 1, 8, tok_h), f32),
            pltpu.VMEM((HALVES, NZ, 8, tok_h), f32),
            pltpu.VMEM((HALVES, tok_h, GW), f32),
            pltpu.VMEM((HALVES, NZ - 1, tok_h, GW), bf),
            pltpu.VMEM((HALVES, NZ - 1, tok_h, GW), bf),
            pltpu.VMEM((HALVES, tok_h, GW), bf),
            pltpu.VMEM(out_weight.shape, bf),
            pltpu.VMEM(gate_table.shape, f32),
            pltpu.VMEM(residual.shape, bf),
            pltpu.VMEM((HALVES, nx, NL, half_rows, n_cols), bf),
            pltpu.VMEM((HALVES, nx - 1, NL, half_rows, n_cols), bf),
            pltpu.VMEM((HALVES, NL, half_rows, n_cols), f32),
            pltpu.VMEM((HALVES, half_rows, n_cols), bf),
            pltpu.VMEM((HALVES, half_rows, n_cols), bf),
            pltpu.VMEM((nx, half_rows, n_cols), bf),
            pltpu.VMEM((nx - 1, half_rows, n_cols), bf),
            pltpu.VMEM((nx - 1, half_rows, n_cols), bf),
            pltpu.SMEM((NZ * 2 * ny,), f32),
            dma(nh), dma(nh), dma(nh), dma(nh), dma(nh), dma(nh), dma(HALVES * NZ), dma(HALVES * NZ),
            *ring,
            dma(HALVES * NZ), dma(HALVES * NZ), dma(HALVES * NZ), dma(HALVES * NZ),
            dma(n_p * nx), dma(n_p * nx), dma(n_p), dma(n_p), dma(6),
        ],
        compiler_params=pltpu.CompilerParams(
            collective_id=0, has_side_effects=True, vmem_limit_bytes=56 * 2**20
        ),
        name="segment_attention",
    )(
        query.reshape(HALVES, half_rows, n_cols), key, value, residual, out_weight, gate_table,
        noise_steps, segment_mask, segment_map,
    )


def solution(mesh):
    nh = mesh.shape["head"]
    ny = mesh.shape["seq"] // (NZ * NC)
    rows = P(("seq", "head"), None)
    return jax.shard_map(
        functools.partial(per_device, ny, nh),
        mesh=mesh,
        in_specs=(rows, rows, rows, rows, P("head", None), P(), P(), P(), P()),
        out_specs=rows,
        check_vma=False,
    )
```
